32 devices in a mesh: gx: 4 (over y, x), gy: 4 (over z), gz: 2 (over core).
Axes of the slice: x: 2, y: 2, z: 4, core: 2. Of those that a mesh axis runs over, the one named last changes fastest.
Arguments:
- state_old: float32 [3, 32, 64, 512], P(None, 'gz', 'gy', 'gx'), may hold values from -6 to 6
- source: float32 [3, 32, 64, 512], P(None, 'gz', 'gy', 'gx'), may hold values from -8 to 8
- volume: float32 [32, 64, 512], P('gz', 'gy', 'gx'), may hold values from 0.5 to 2
- perm: float32 [3, 32, 64, 512], P(None, 'gz', 'gy', 'gx'), may hold values from 0.3 to 3
- coupling: float32 [6, 32, 64, 512], P(None, 'gz', 'gy', 'gx'), may hold values from -0.25 to 0.25
- mobility: float32 [3, 32, 64, 512], P(None, 'gz', 'gy', 'gx'), may hold values from 0.2 to 1
- send_cell: int32 [4, 8, 32], P('gx', ('gy', 'gz')), may hold values from -1 to 32767, as said below
- send_wi: float32 [4, 8, 32], P('gx', ('gy', 'gz')), may hold values from 0.3 to 2
- recv_well: int32 [4, 8, 32], P('gx', ('gy', 'gz')), may hold values from -1 to 15, as said below
- controls: int32 [4, 8, 2, 16], P('gx', ('gy', 'gz')), may hold values 0 or 1
- inner_iters: int32 [2], replicated, may hold values from 2 to 8, as said below
- well_target: float32 [4, 8, 16], P('gx', ('gy', 'gz')), may hold values from -6 to 6
- well_rate: float32 [4, 8, 16], P('gx', ('gy', 'gz')), may hold values from -6 to 6
- well_store: float32 [4, 8, 16], P('gx', ('gy', 'gz')), may hold values from 0.2 to 1
- well_pressure: float32 [4, 8, 16], P('gx', ('gy', 'gz')), may hold values from -6 to 6
Outputs:
- cell_state: float32 [3, 32, 64, 512], P(None, 'gz', 'gy', 'gx')
- well_bhp: float32 [4, 8, 16], P('gx', ('gy', 'gz'))
The draws below stay inside these ranges and needn't reach their ends.
Inputs may be any that keep to these rules, and one draw needn't show every extreme that they name: `send_cell`: each block of 4 entries (one block a manager of the group) lists distinct local cells of the device, live entries first, then -1; every block holds at least one live entry, and in each gx group one manager receives 4 live entries from every device. `recv_well`: entry s * 4 + k is -1 exactly where entry d * 4 + k of send_cell[a, s] is -1, else a well of manager (a, d). `inner_iters`: at least one Newton iteration takes 8 inner iterations.
All inputs are finite; a program needn't handle non-finite values. No bound on the sum of `controls` on one device may be relied on, other than what follows from the above.
Results may differ from the reference program's by a relative error of at most 0.0003.
Values sent between devices are 32-bit elements; how exact they have to be, the bound alone decides.
A program may use at most 128 MiB of HBM per device.

```python
import math
import jax
import jax.numpy as jnp
from jax import lax

CX = 128
CY = 16
CZ = 16
WELL_DEV = 16
CAP = 4
NEWTON = 2
ITMAX = 8
GROUPS = 4
PEERS = 8
CELLS = 32768
NX = 512
NY = 64
NZ = 32
N_GX = 4
N_GY = 4
N_GZ = 2


def slot_layout(key):
    base = jax.random.fold_in(key, 11)
    keys = jax.random.split(base, 4)
    counts = jax.random.randint(keys[0], (GROUPS, PEERS, PEERS), 1, CAP + 1)
    chosen = jax.random.randint(keys[1], (GROUPS,), 0, PEERS)
    counts = jnp.where(jnp.arange(PEERS)[None, None, :] == chosen[:, None, None], CAP, counts)
    live = jnp.arange(CAP)[None, None, None, :] < counts[..., None]
    cell_keys = jax.random.split(keys[2], GROUPS * PEERS)
    picked = jax.vmap(lambda k: jax.random.permutation(k, CELLS)[:PEERS * CAP])(cell_keys)
    picked = picked.reshape(GROUPS, PEERS, PEERS, CAP).astype(jnp.int32)
    wells = jax.random.randint(keys[3], (GROUPS, PEERS, PEERS, CAP), 0, WELL_DEV)
    sender = jnp.where(live, picked, -1).reshape(GROUPS, PEERS, PEERS * CAP)
    receiver = jnp.where(live, wells, -1).transpose(0, 2, 1, 3).reshape(GROUPS, PEERS, PEERS * CAP)
    return (sender.astype(jnp.int32), receiver.astype(jnp.int32))


def draw_send_cell(key, part):
    return slot_layout(key)[0]


def draw_recv_well(key, part):
    return slot_layout(key)[1]


def draw_inner_iters(key, part):
    values = jax.random.randint(jax.random.fold_in(key, 5), (NEWTON,), ITMAX // 4, ITMAX + 1)
    chosen = jax.random.randint(jax.random.fold_in(key, 6), (), 0, NEWTON)
    return jnp.where(jnp.arange(NEWTON) == chosen, ITMAX, values).astype(jnp.int32)


def draw_source(key, part):
    keys = jax.random.split(jax.random.fold_in(key, 21), 2)
    phase = jax.random.uniform(keys[0], (3, 1, 1, 1), jnp.float32, 0.0, 2.0 * jnp.pi)
    xs = (jnp.arange(NX, dtype=jnp.float32) + 0.5) / NX
    ys = (jnp.arange(NY, dtype=jnp.float32) + 0.5) / NY
    zs = (jnp.arange(NZ, dtype=jnp.float32) + 0.5) / NZ
    wave = 1.0 + 0.4 * jnp.sin(2.0 * jnp.pi * xs[None, None, None, :] + phase) * jnp.cos(2.0 * jnp.pi * ys[None, None, :, None]) + 0.1 * jnp.cos(jnp.pi * zs[None, :, None, None])
    level = jnp.array([2.0, -1.0, 1.0], jnp.float32).reshape(3, 1, 1, 1)
    rough = jnp.clip(jax.random.normal(keys[1], (3, NZ, NY, NX), jnp.float32), -4.0, 4.0)
    return (level * wave + rough).astype(jnp.float32)


def plant(result, key, smallest, largest):
    longest = result.shape.index(max(result.shape))
    spots = []
    for shift in (0, 1):
        where = [jax.random.randint(jax.random.fold_in(key, axis), (), 0, length) for axis, length in enumerate(result.shape)]
        where[longest] = (where[longest] + shift) % result.shape[longest]
        spots.append(tuple(where))
    return result.at[spots[0]].set(smallest).at[spots[1]].set(largest)


def steps_of(key, shape, pieces, least, largest):
    gain = 1.0
    for axis_at, shards_of in pieces:
        draws = jax.random.uniform(jax.random.fold_in(jax.random.fold_in(key, 6), axis_at), (shards_of,), jnp.float32, least / len(pieces), largest / len(pieces))
        gain = gain * jnp.repeat(jnp.exp(draws), shape[axis_at] // shards_of).reshape((-1,) + (1,) * (len(shape) - 1 - axis_at))
    return gain


def gaussian(rng, shape, spread, reach, pieces=(), kind=jnp.bfloat16):
    loudness = steps_of(rng, shape, pieces, -0.22, 0.18) if pieces else 1.0
    values = jax.random.normal(rng, shape, jnp.float32) * spread * loudness
    return jnp.minimum(jnp.maximum(values, -reach), reach).astype(kind)


def setup_inputs(seed: int = 0) -> dict:
    streams_of = jax.random.split(jax.random.key(seed), 16)
    return {
        "state_old": gaussian(streams_of[0], (3, NZ, NY, NX), 1.0, 6.0, ((1, 2), (2, 4), (3, 4)), jnp.float32),
        "source": draw_source(jax.random.fold_in(streams_of[15], 71), 0),
        "volume": jnp.clip(jnp.exp(math.log(2.0) - 1.3862944 * jax.random.uniform(streams_of[2], (NZ, NY, NX), jnp.float32) ** steps_of(streams_of[2], (NZ, NY, NX), ((0, 2), (1, 4), (2, 4)), -0.2, 0.2)), 0.5, 2.0),
        "perm": jnp.clip(jnp.exp(math.log(3.0) - 2.3025851 * jax.random.uniform(streams_of[3], (3, NZ, NY, NX), jnp.float32) ** steps_of(streams_of[3], (3, NZ, NY, NX), ((1, 2), (2, 4), (3, 4)), -0.2, 0.2)), 0.3, 3.0),
        "coupling": jnp.clip(jax.random.uniform(streams_of[4], (6, NZ, NY, NX), jnp.float32, -0.25, 0.25) * steps_of(streams_of[4], (6, NZ, NY, NX), ((1, 2), (2, 4), (3, 4)), -0.4, 0.0), -0.25, 0.25),
        "mobility": jnp.clip(jnp.exp(math.log(1.0) - 1.609438 * jax.random.uniform(streams_of[5], (3, NZ, NY, NX), jnp.float32) ** steps_of(streams_of[5], (3, NZ, NY, NX), ((1, 2), (2, 4), (3, 4)), -0.2, 0.2)), 0.2, 1.0),
        "send_cell": draw_send_cell(jax.random.fold_in(streams_of[15], 71), 0),
        "send_wi": jnp.clip(jnp.exp(math.log(2.0) - 1.89712 * jax.random.uniform(streams_of[7], (GROUPS, PEERS, PEERS * CAP), jnp.float32) ** steps_of(streams_of[7], (GROUPS, PEERS, PEERS * CAP), ((0, 4), (1, 8)), -0.2, 0.2)), 0.3, 2.0),
        "recv_well": draw_recv_well(jax.random.fold_in(streams_of[15], 71), 0),
        "controls": plant((jax.random.randint(streams_of[9], (GROUPS, PEERS, NEWTON, WELL_DEV), 0, 2) < 1).astype(jnp.int32), jax.random.fold_in(streams_of[9], 1), 0, 1),
        "inner_iters": draw_inner_iters(jax.random.fold_in(streams_of[15], 71), 0),
        "well_target": gaussian(streams_of[11], (GROUPS, PEERS, WELL_DEV), 1.0, 6.0, ((0, 4), (1, 8)), jnp.float32),
        "well_rate": gaussian(streams_of[12], (GROUPS, PEERS, WELL_DEV), 1.0, 6.0, ((0, 4), (1, 8)), jnp.float32),
        "well_store": jnp.clip(jnp.exp(math.log(1.0) - 1.609438 * jax.random.uniform(streams_of[13], (GROUPS, PEERS, WELL_DEV), jnp.float32) ** steps_of(streams_of[13], (GROUPS, PEERS, WELL_DEV), ((0, 4), (1, 8)), -0.2, 0.2)), 0.2, 1.0),
        "well_pressure": gaussian(streams_of[14], (GROUPS, PEERS, WELL_DEV), 1.0, 6.0, ((0, 4), (1, 8)), jnp.float32),
    }


couple_pairs = ((0, 1), (0, 2), (1, 0), (1, 2), (2, 0), (2, 1))


def neighbours(padded):
    return [padded[:, 1:-1, 1:-1, 2:], padded[:, 1:-1, 1:-1, :-2],
            padded[:, 1:-1, 2:, 1:-1], padded[:, 1:-1, :-2, 1:-1],
            padded[:, 2:, 1:-1, 1:-1], padded[:, :-2, 1:-1, 1:-1]]


def face_weights(perm, padded):
    near = neighbours(padded)
    weights = []
    for facet in range(6):
        own = perm[facet // 2]
        other = near[facet][facet // 2]
        weights.append(2.0 * own * other / (own + other))
    return weights


def gathered(weights, near):
    total = weights[0] * near[0]
    for facet in range(1, 6):
        total = total + weights[facet] * near[facet]
    return total


def mixing(coupling, vector):
    rows = [vector[0], vector[1], vector[2]]
    for position, pair in enumerate(couple_pairs):
        rows[pair[0]] = rows[pair[0]] + coupling[position] * vector[pair[1]]
    return jnp.stack(rows)


def storage(values):
    return values + 0.5 * jnp.tanh(values)


def block_matrix(coupling, total_weight, volume, current, wi_cell, mobility):
    hyper = jnp.tanh(current)
    slope = 1.0 + 0.5 * (1.0 - hyper * hyper)
    matrix = [[None, None, None], [None, None, None], [None, None, None]]
    for row in range(3):
        matrix[row][row] = total_weight + volume * slope[row]
    for position, pair in enumerate(couple_pairs):
        matrix[pair[0]][pair[1]] = total_weight * coupling[position]
    for row in range(3):
        matrix[row][0] = matrix[row][0] + wi_cell * mobility[row]
    return matrix


def minor(matrix, row, col):
    keep_rows = [r for r in range(3) if r != row]
    keep_cols = [c for c in range(3) if c != col]
    return (matrix[keep_rows[0]][keep_cols[0]] * matrix[keep_rows[1]][keep_cols[1]]
            - matrix[keep_rows[0]][keep_cols[1]] * matrix[keep_rows[1]][keep_cols[0]])


def invert(matrix):
    cofac = [[(1.0 if (r + c) % 2 == 0 else -1.0) * minor(matrix, r, c) for c in range(3)] for r in range(3)]
    determinant = matrix[0][0] * cofac[0][0] + matrix[0][1] * cofac[0][1] + matrix[0][2] * cofac[0][2]
    factor = 1.0 / determinant
    return [[cofac[c][r] * factor for c in range(3)] for r in range(3)]


def solve_block(inverse, vector):
    return jnp.stack([inverse[r][0] * vector[0] + inverse[r][1] * vector[1] + inverse[r][2] * vector[2] for r in range(3)])


def padded_of(field):
    return jnp.pad(field, ((0, 0), (1, 1), (1, 1), (1, 1)))


def tile(field):
    depth = field.shape[0]
    shaped = field.reshape(depth, N_GZ, CZ, N_GY, CY, N_GX, CX)
    return shaped.transpose(5, 3, 1, 0, 2, 4, 6).reshape(GROUPS, PEERS, depth, CELLS)


def untile(tiles):
    depth = tiles.shape[2]
    shaped = tiles.reshape(N_GX, N_GY, N_GZ, depth, CZ, CY, CX)
    return shaped.transpose(3, 2, 4, 1, 5, 0, 6).reshape(depth, NZ, NY, NX)


def reference(state_old, source, volume, perm, coupling, mobility, send_cell, send_wi, recv_well,
              controls, inner_iters, well_target, well_rate, well_store, well_pressure):
    weights = face_weights(perm, padded_of(perm))
    total_weight = weights[0]
    for facet in range(1, 6):
        total_weight = total_weight + weights[facet]
    live = send_cell >= 0
    slot_cell = jnp.maximum(send_cell, 0).astype(jnp.int32)
    wi_slot = jnp.where(live, send_wi, jnp.float32(0.0))
    flat_cells = (jnp.arange(GROUPS * PEERS, dtype=jnp.int32)[:, None] * CELLS
                  + slot_cell.reshape(GROUPS * PEERS, PEERS * CAP)).reshape(-1)

    def cell_add(values):
        summed = jnp.zeros((GROUPS * PEERS * CELLS,), jnp.float32).at[flat_cells].add(values.reshape(-1))
        return untile(summed.reshape(GROUPS, PEERS, 1, CELLS))[0]

    def pick(field):
        return jnp.take_along_axis(tile(field[None])[:, :, 0, :], slot_cell, axis=2)

    def flip(slots):
        return slots.reshape(GROUPS, PEERS, PEERS, CAP).transpose(0, 2, 1, 3).reshape(GROUPS, PEERS, PEERS * CAP)

    onehot = (recv_well[..., None] == jnp.arange(WELL_DEV, dtype=jnp.int32)).astype(jnp.float32)

    def well_sum(owner_slots):
        return jnp.einsum("gds,gdsw->gdw", flip(owner_slots), onehot, precision=lax.Precision.HIGHEST)

    def to_slots(wells):
        return flip(jnp.einsum("gdsw,gdw->gds", onehot, wells, precision=lax.Precision.HIGHEST))

    mob_total = mobility[0] + mobility[1] + mobility[2]
    slot_coef = wi_slot * pick(mob_total)
    wi_cell = cell_add(wi_slot)
    rate_sum = well_sum(slot_coef)
    current = state_old
    pressure = well_pressure
    for newton in range(NEWTON):
        control = controls[:, :, newton, :].astype(jnp.float32)
        near_state = neighbours(padded_of(current))
        slot_pressure = pick(current[0])
        weighted = well_sum(slot_coef * slot_pressure)
        inflow = cell_add(wi_slot * (slot_pressure - to_slots(pressure)))
        residual = (volume * (storage(current) - storage(state_old))
                    + mixing(coupling, total_weight * current - gathered(weights, near_state))
                    + mobility * inflow - source)
        well_res = ((1.0 - control) * (pressure - well_target)
                    + control * (well_store * (pressure - well_pressure) + pressure * rate_sum - weighted + well_rate))
        well_diag = (1.0 - control) + control * (well_store + rate_sum)
        inverse = invert(block_matrix(coupling, total_weight, volume, current, wi_cell, mobility))

        def sweep(turn, carry):
            update, well_update = carry
            linked = cell_add(wi_slot * to_slots(well_update))
            near_update = neighbours(padded_of(update))
            rhs = -residual + mixing(coupling, gathered(weights, near_update)) + mobility * linked
            new_update = solve_block(inverse, rhs)
            new_well = (-well_res + control * well_sum(slot_coef * pick(update[0]))) / well_diag
            return new_update, new_well

        update, well_update = lax.fori_loop(0, inner_iters[newton], sweep,
                                            (jnp.zeros_like(current), jnp.zeros_like(pressure)))
        current = current + update
        pressure = pressure + well_update
    return current, pressure
```

```python
import functools

import jax
import jax.numpy as jnp
from jax import lax
from jax.experimental import pallas as pl
from jax.experimental.pallas import tpu as pltpu
from jax.sharding import PartitionSpec as P

NEWTON = 2
ITMAX = 8
PAIRS = ((0, 1), (0, 2), (1, 0), (1, 2), (2, 0), (2, 1))
F32 = jnp.float32
GDEPTH = 4


def iota(shape, dim):
    return lax.broadcasted_iota(jnp.int32, shape, dim)


def each(count, body):
    if count <= 8:
        for i in range(count):
            body(i)
    else:
        lax.fori_loop(0, count, lambda i, c: (body(i), c)[1], 0)


def kernel(cfg, state, source, volume, perm, coupling, mobility, small, controls, iters, wtarget,
           wrate, wstore, wpress, u, bhp,
           txp, typ, tz, tzh, tyh, tpk, total, nu, cc, mm, ww, du, nloc, lfield, wcell,
           hx, hy, hz, px, py, pz, sx, sy, spx, spy,
           gbuf, gsend, ginit, ginit_send, raw, raw_send, qbuf, eqb, gkeep,
           hsend, hrecv, gss, grs, iss, irs):
    ngx, ngy, ngz, nz, ny, nx, slots, wells, turns = cfg
    peers = ngy * ngz
    cap = slots // peers
    rows = nz * ny
    half = ny // 8
    per = rows // 8
    tiles = small.shape[0] // 8
    width = min(slots, 128)
    gx, gy, gz = lax.axis_index("gx"), lax.axis_index("gy"), lax.axis_index("gz")
    me = gy * ngz + gz
    lane8 = iota((8, 128), 1)
    sub8 = iota((8, 128), 0)
    lane_p = iota((ny, 128), 1)
    sub_p = iota((ny, 128), 0)
    edge = (lane8 == 0) | (lane8 == 127)
    odd = (lane8 % 2) == 1

    def peer_id(t):
        return {"gy": t // ngz, "gz": t % ngz}

    barrier = pltpu.get_barrier_semaphore()

    def greet(o):
        pl.semaphore_signal(barrier, inc=1, device_id=peer_id((me + o + 1) % peers),
                            device_id_type=pl.DeviceIdType.MESH)

    zeros_h = jnp.zeros((3 * ny, 128), F32)
    for slot in range(3):
        for side in range(2):
            hz[slot, side] = zeros_h.reshape(3, ny, 128)
            hy[slot, side] = jnp.zeros((3 * nz, 128), F32)
            hx[slot, side] = jnp.zeros((16, 128), F32)
    for side in range(2):
        px[side] = jnp.zeros((8, 128), F32)
        py[side] = jnp.zeros((nz, 128), F32)
        pz[side] = jnp.zeros((ny, 128), F32)

    each(peers - 1, greet)

    @pl.when(gx > 0)
    def _():
        pl.semaphore_signal(barrier, inc=1, device_id={"gx": gx - 1}, device_id_type=pl.DeviceIdType.MESH)

    @pl.when(gx < ngx - 1)
    def _():
        pl.semaphore_signal(barrier, inc=1, device_id={"gx": gx + 1}, device_id_type=pl.DeviceIdType.MESH)

    conds = (gx < ngx - 1, gx > 0, gy < ngy - 1, gy > 0, gz < ngz - 1, gz > 0)
    gets = (gx > 0, gx < ngx - 1, gy > 0, gy < ngy - 1, gz > 0, gz < ngz - 1)
    where_to = ({"gx": gx + 1}, {"gx": gx - 1}, {"gy": gy + 1}, {"gy": gy - 1},
                {"gz": gz + 1}, {"gz": gz - 1})

    def remote(src, dst, ss, rs, dev):
        return pltpu.make_async_remote_copy(src_ref=src, dst_ref=dst, send_sem=ss, recv_sem=rs,
                                            device_id=dev, device_id_type=pl.DeviceIdType.MESH)

    def halo(slot, cells):
        top = pl.ds(rows - ny, ny)
        srcs = (sx.at[slot], sx.at[slot], sy.at[slot, 1], sy.at[slot, 0],
                cells.at[:, top, :], cells.at[:, pl.ds(0, ny), :])
        dsts = (hx.at[slot, 0], hx.at[slot, 1], hy.at[slot, 0], hy.at[slot, 1],
                hz.at[slot, 0], hz.at[slot, 1])
        return [remote(srcs[i], dsts[i], hsend.at[slot, i], hrecv.at[slot, i], where_to[i])
                for i in range(6)]

    def perm_halo():
        top = pl.ds(rows - ny, ny)
        srcs = (spx, spx, spy.at[1], spy.at[0], perm.at[2, top, :], perm.at[2, pl.ds(0, ny), :])
        dsts = (px.at[0], px.at[1], py.at[0], py.at[1], pz.at[0], pz.at[1])
        return [remote(srcs[i], dsts[i], hsend.at[3, i], hrecv.at[3, i], where_to[i])
                for i in range(6)]

    order = (0, 1, 2, 3, 4, 5)

    def start(copies):
        for i in order:
            pl.when(conds[i])(copies[i].start)

    def finish(copies):
        for i in order:
            pl.when(gets[i])(copies[i].wait_recv)
        for i in order:
            pl.when(conds[i])(copies[i].wait_send)

    def spread(src, dst_of, ss, rs, act):
        def one(o):
            o = o + 1
            if act == "start":
                remote(src, dst_of(me), ss(o), rs(o), peer_id((me + o) % peers)).start()
            else:
                got = remote(src, dst_of((me + peers - o) % peers), ss(o), rs(o),
                             peer_id((me + o) % peers))
                got.wait_recv()
                got.wait_send()
        each(peers - 1, one)

    def grow(slot):
        return lambda t: gbuf.at[pl.ds(pl.multiple_of((slot * peers + t) * 8, 8), 8), :]

    def gcopy(slot, act):
        spread(gsend.at[slot], grow(slot), lambda o: gss.at[slot, o], lambda o: grs.at[slot, o], act)

    def icopy(act):
        spread(ginit_send, lambda t: ginit.at[pl.ds(pl.multiple_of(t * 8, 8), 8), :],
               lambda o: iss.at[0, o], lambda o: irs.at[0, o], act)

    def rcopy(act):
        spread(raw_send, lambda t: raw.at[pl.ds(pl.multiple_of(t * 8 * tiles, 8), 8 * tiles), :],
               lambda o: iss.at[1, o], lambda o: irs.at[1, o], act)

    def pack(acc, value, j):
        return jnp.where(lane8 // 2 == j, pltpu.roll(value, 2 * j + 1, 1), acc)

    def unpack(acc, j):
        return jnp.where(edge, pltpu.roll(acc, 127 - 2 * j, 1), 0.0)

    def face(left, right):
        return jnp.where(odd, pltpu.roll(left, 1, 1), pltpu.roll(right, 127, 1))

    def spot(c, z, h):
        return (0, c * per + z * half + h) if c < 2 else (1, z * half + h)

    def pack_field(read):
        def body(z, acc):
            acc = list(acc)
            for c in range(3):
                for h in range(half):
                    t, j = spot(c, z, h)
                    acc[t] = pack(acc[t], read(c, pl.multiple_of(z * ny + h * 8, 8)), j)
            return tuple(acc)
        z0 = jnp.zeros((8, 128), F32)
        return lax.fori_loop(0, nz, body, (z0, z0), unroll=2)

    def put_y(slot, read):
        for c in range(3):
            sy[slot, 0, pl.ds(c * nz, nz), :] = read(c, 0)
            sy[slot, 1, pl.ds(c * nz, nz), :] = read(c, ny - 1)

    a0, a1 = pack_field(lambda c, r: state[c, pl.ds(r, 8), :])
    sx[2] = jnp.concatenate([a0, a1], 0)

    def perm_body(z, acc):
        for h in range(half):
            acc = pack(acc, perm[0, pl.ds(pl.multiple_of(z * ny + h * 8, 8), 8), :], z * half + h)
        return acc
    own_px = lax.fori_loop(0, nz, perm_body, jnp.zeros((8, 128), F32), unroll=2)
    spx[...] = own_px
    put_y(2, lambda c, y: state[c, pl.ds(y, nz, stride=ny), :])
    spy[0] = perm[1, pl.ds(0, nz, stride=ny), :]
    spy[1] = perm[1, pl.ds(ny - 1, nz, stride=ny), :]

    cell_row = [small[pl.ds(8 * t, 1), :] for t in range(tiles)]
    wi_row = [jnp.where(cell_row[t] >= 0, small[pl.ds(8 * t + 1, 1), :], 0.0) for t in range(tiles)]
    rw_row = [small[pl.ds(8 * t + 2, 1), :] for t in range(tiles)]
    diag = iota((width, 128), 0) == iota((width, 128), 1)

    def to_col(row):
        return jnp.sum(jnp.where(diag, row, 0.0), axis=1, keepdims=True)

    def to_row(col):
        return jnp.sum(jnp.where(diag, col, 0.0), axis=0, keepdims=True)

    for t in range(tiles):
        out = rw_row[t]
        block = jnp.where(sub8 == 0, out, 0.0)
        for w in range(wells):
            here = out == float(w)
            vals = (controls[0, 0, 0, w].astype(F32), controls[0, 0, 1, w].astype(F32),
                    wtarget[0, 0, w], wrate[0, 0, w], wstore[0, 0, w], wpress[0, 0, w])
            col = jnp.zeros((8, 128), F32)
            for p, v in enumerate(vals):
                col = jnp.where(sub8 == p + 1, v, col)
            block = jnp.where(here & (sub8 > 0), col, block)
        raw_send[pl.ds(8 * t, 8), :] = block
        raw[pl.ds(pl.multiple_of((me * tiles + t) * 8, 8), 8), :] = block

    if ngx > 2:
        inner = (gx > 0) & (gx < ngx - 1)

        @pl.when(inner)
        def _():
            pl.semaphore_wait(barrier, peers + 1)

        @pl.when(jnp.logical_not(inner))
        def _():
            pl.semaphore_wait(barrier, peers)
    else:
        pl.semaphore_wait(barrier, peers - 2 + ngx)

    pcopies = perm_halo()
    start(pcopies)
    start(halo(2, state))
    rcopy("start")

    hot, lanes_hot, hot_t = [], [], []
    for t in range(tiles):
        col = to_col(cell_row[t]).astype(jnp.int32)
        col_row = jnp.where(col >= 0, col // nx, -1)
        col_lane = jnp.where(col >= 0, col % nx, -1)
        row_i = cell_row[t][:, :width].astype(jnp.int32)
        row_row = jnp.where(row_i >= 0, row_i // nx, -1)
        hot.append((iota((width, rows), 1) == col_row).astype(jnp.bfloat16))
        lanes_hot.append((iota((width, 128), 1) == col_lane).astype(F32))
        hot_t.append((iota((rows, width), 0) == row_row).astype(jnp.bfloat16))

    def pick(field):
        hi = field.astype(jnp.bfloat16)
        lo = (field - hi.astype(F32)).astype(jnp.bfloat16)
        out = []
        for t in range(tiles):
            got = (jnp.dot(hot[t], hi, preferred_element_type=F32)
                   + jnp.dot(hot[t], lo, preferred_element_type=F32))
            out.append(to_row(jnp.sum(got * lanes_hot[t], axis=1, keepdims=True)))
        return out

    def scatter(vals):
        total_ = jnp.zeros((rows, 128), F32)
        for t in range(tiles):
            full = to_col(vals[t]) * lanes_hot[t]
            hi = full.astype(jnp.bfloat16)
            lo = (full - hi.astype(F32)).astype(jnp.bfloat16)
            total_ = (total_ + jnp.dot(hot_t[t], hi, preferred_element_type=F32)
                      + jnp.dot(hot_t[t], lo, preferred_element_type=F32))
        return total_

    def share(vals, send, rows_at):
        block = jnp.zeros((8, 128), F32)
        for t in range(tiles):
            block = jnp.where(sub8 == t, vals[t], block)
        send[...] = block
        rows_at[...] = block

    coef = [wi_row[t] * v for t, v in enumerate(pick(mobility[0] + mobility[1] + mobility[2]))]
    share(coef, ginit_send, ginit.at[pl.ds(pl.multiple_of(me * 8, 8), 8), :])
    icopy("start")
    u0s = pick(state[0])
    share([coef[t] * u0s[t] for t in range(tiles)], gsend.at[0], grow(0)(me))
    gcopy(0, "start")
    wcell[...] = scatter(wi_row)

    def tface(a, b):
        return 2.0 * a * b / (a + b)

    for c in range(3):
        u[c] = state[c]
    tz[pl.ds(0, ny), :] = jnp.zeros((ny, 128), F32)
    tz[pl.ds(rows, ny), :] = jnp.zeros((ny, 128), F32)

    def weights_body(z, carry):
        at = pl.ds(pl.multiple_of(z * ny, 8), ny)
        k0, k1 = perm[0, at, :], perm[1, at, :]
        txp[at, :] = jnp.where(lane_p == 127, 0.0, tface(k0, pltpu.roll(k0, 127, 1)))
        typ[at, :] = jnp.where(sub_p == ny - 1, 0.0, tface(k1, pltpu.roll(k1, ny - 1, 0)))
        return carry
    lax.fori_loop(0, nz, weights_body, 0, unroll=2)

    def tz_body(z, carry):
        at = pl.ds(pl.multiple_of(z * ny, 8), ny)
        before = pl.ds(pl.multiple_of(z * ny - ny, 8), ny)
        tz[at, :] = tface(perm[2, before, :], perm[2, at, :])
        return carry
    lax.fori_loop(1, nz, tz_body, 0, unroll=3)

    def local_plane(read, z, low, high):
        at = pl.ds(pl.multiple_of(z * ny, 8), ny)
        above = pl.ds(pl.multiple_of(z * ny + ny, 8), ny)
        wx, wy = txp[at, :], typ[at, :]
        for c in range(3):
            v = read(c, at)
            n = wx * pltpu.roll(v, 127, 1) + pltpu.roll(wx * v, 1, 1)
            n = n + (wy * pltpu.roll(v, ny - 1, 0) + pltpu.roll(wy * v, 1, 0))
            if low:
                below = pl.ds(pl.multiple_of(z * ny - ny, 8), ny)
                n = n + tz[at, :] * read(c, below)
            if high:
                n = n + tz[above, :] * read(c, above)
            nloc[c, at, :] = n

    def local(read):
        local_plane(read, 0, False, True)
        lax.fori_loop(1, nz - 1, lambda z, c: (local_plane(read, z, True, True), c)[1], 0, unroll=2)
        local_plane(read, nz - 1, True, False)

    def halo_z(slot):
        lo, hi = pl.ds(0, ny), pl.ds(rows - ny, ny)
        for c in range(3):
            nloc[c, lo, :] = nloc[c, lo, :] + tzh[0] * hz[slot, 0, c]
            nloc[c, hi, :] = nloc[c, hi, :] + tzh[1] * hz[slot, 1, c]

    def halo_x(slot):
        return [tpk[t] * face(hx[slot, 0, pl.ds(8 * t, 8), :], hx[slot, 1, pl.ds(8 * t, 8), :])
                for t in range(2)]

    def with_halo(slot, xs, c, z, h):
        r = pl.ds(pl.multiple_of(z * ny + h * 8, 8), 8)
        n = nloc[c, r, :]
        t, j = spot(c, z, h)
        n = n + unpack(xs[t], j)
        if h == 0:
            lo = tyh[0, pl.ds(z, 1), :] * hy[slot, 0, pl.ds(c * nz + z, 1), :]
            n = n + jnp.where(sub8 == 0, lo, 0.0)
        if h == half - 1:
            hi = tyh[1, pl.ds(z, 1), :] * hy[slot, 1, pl.ds(c * nz + z, 1), :]
            n = n + jnp.where(sub8 == 7, hi, 0.0)
        return n

    local(lambda c, at: state[c, at, :])

    rcopy("wait")

    def turned(s, t):
        acc = jnp.zeros((8, 128), F32)
        per_tile = 128 // cap
        for d in range(t * per_tile, min(peers, (t + 1) * per_tile)):
            src = raw[pl.ds(pl.multiple_of((d * tiles + s // per_tile) * 8, 8), 8), :]
            shift = (cap * (d % per_tile) + 128 - cap * (s % per_tile)) % 128
            acc = jnp.where(lane8 // cap == d % per_tile, pltpu.roll(src, shift, 1), acc)
        return acc

    par = []
    for t in range(tiles):
        def row_of(s, t=t):
            qbuf[pl.ds(t * peers + s, 1), :] = turned(s, t)[0:1]
        each(peers, row_of)
        par.append(turned(me, t))
    lane_g = iota((peers, 128), 1)
    for t in range(tiles):
        q = qbuf[pl.ds(t * peers, peers), :]
        own = par[t][0:1]
        for j in range(-(cap - 1), cap):
            inside = (lane_g % cap + j >= 0) & (lane_g % cap + j < cap)
            same = pltpu.roll(q, (-j) % 128, 1) == own
            eqb[t, j + cap - 1] = jnp.where(inside & same, 1.0, 0.0)

    def read_g(ref, base, t):
        return ref[pl.ds(base + t, peers, stride=8), :]

    def kept(t):
        return gkeep[pl.ds(t * peers, peers), :]

    def same_well(read):
        out = []
        for t in range(tiles):
            g = read(t)
            acc = eqb[t, cap - 1] * g
            for j in range(-(cap - 1), cap):
                if j:
                    acc = acc + eqb[t, j + cap - 1] * pltpu.roll(g, (-j) % 128, 1)
            out.append(jnp.sum(acc, axis=0, keepdims=True))
        return out

    well_sub = iota((wells, 128), 0)
    per_tile = 128 // cap

    def own_wells(read):
        rows_out = jnp.zeros((wells, 128), F32)
        for t in range(tiles):
            g = read(t)
            q = qbuf[pl.ds(t * peers, peers), :]
            mine = (lane_g // cap) == (me - t * per_tile)
            g = jnp.where(mine, g, 0.0)
            for w in range(wells):
                line = jnp.sum(jnp.where(q == float(w), g, 0.0), axis=0, keepdims=True)
                rows_out = rows_out + jnp.where(well_sub == w, line, 0.0)
        return jnp.sum(rows_out, axis=1, keepdims=True)

    def well_col(read):
        col = jnp.zeros((wells, 128), F32)
        for w in range(wells):
            col = jnp.where(well_sub == w, read(w), col)
        return col[:, 0:1]

    tgt_w, rate_w = well_col(lambda w: wtarget[0, 0, w]), well_col(lambda w: wrate[0, 0, w])
    store_w, p0_w = well_col(lambda w: wstore[0, 0, w]), well_col(lambda w: wpress[0, 0, w])

    def parts(f, pw, tgt, rate, store, p0, rsum):
        e = (1.0 - f) * (pw - tgt) + f * (store * (pw - p0) + pw * rsum + rate)
        dw = 1.0 - f + f * (store + rsum)
        return -e / dw, f / dw

    icopy("wait")
    rsum_s = same_well(lambda t: read_g(ginit, 0, t))
    rsum_w = own_wells(lambda t: read_g(ginit, 0, t))
    gkeep[...] = jnp.zeros((tiles * peers, 128), F32)
    tgt_s, rate_s = [p[3:4] for p in par], [p[4:5] for p in par]
    store_s, p0_s = [p[5:6] for p in par], [p[6:7] for p in par]
    pw_s, pw_w = list(p0_s), p0_w

    finish(pcopies)
    lo_z, hi_z = pl.ds(0, ny), pl.ds(rows - ny, ny)
    tzh[0] = tface(perm[2, lo_z, :], pz[0])
    tzh[1] = tface(perm[2, hi_z, :], pz[1])
    tyh[0] = tface(spy[0], py[0])
    tyh[1] = tface(spy[1], py[1])
    near = face(px[0], px[1])
    used = lane8 < 2 * per
    tp = jnp.where(used, tface(jnp.where(used, own_px, 1.0), near), 0.0)
    tpk[1] = tp
    tpk[0] = tp + pltpu.roll(tp, 2 * per, 1)

    def total_body(z, carry):
        at = pl.ds(pl.multiple_of(z * ny, 8), ny)
        above = pl.ds(pl.multiple_of(z * ny + ny, 8), ny)
        wx, wy = txp[at, :], typ[at, :]
        s = wx + pltpu.roll(wx, 1, 1) + wy + pltpu.roll(wy, 1, 0) + tz[at, :] + tz[above, :]
        s = s + jnp.where(sub_p == 0, tyh[0, pl.ds(z, 1), :], 0.0)
        s = s + jnp.where(sub_p == ny - 1, tyh[1, pl.ds(z, 1), :], 0.0)
        total[at, :] = s
        for h in range(half):
            r = pl.ds(pl.multiple_of(z * ny + h * 8, 8), 8)
            total[r, :] = total[r, :] + unpack(tp, z * half + h)
        return carry
    lax.fori_loop(0, nz, total_body, 0, unroll=2)
    total[lo_z, :] = total[lo_z, :] + tzh[0]
    total[hi_z, :] = total[hi_z, :] + tzh[1]

    finish(halo(2, state))

    def add_to_nu(slot, first):
        halo_z(slot)
        xs = halo_x(slot)

        def body(z, carry):
            for c in range(3):
                for h in range(half):
                    r = pl.ds(pl.multiple_of(z * ny + h * 8, 8), 8)
                    n = with_halo(slot, xs, c, z, h)
                    nu[c, r, :] = n if first else nu[c, r, :] + n
            return carry
        lax.fori_loop(0, nz, body, 0, unroll=2)

    add_to_nu(2, True)

    def setup(first, slot):
        lfield[...] = scatter([wi_row[t] * (u0s[t] - pw_s[t]) for t in range(tiles)])

        def body(z, acc):
            acc = list(acc)
            for h in range(half):
                r = pl.ds(pl.multiple_of(z * ny + h * 8, 8), 8)
                s, vol, wc, q = total[r, :], volume[r, :], wcell[r, :], lfield[r, :]
                cp = [coupling[i, r, :] for i in range(6)]
                mob = [mobility[i, r, :] for i in range(3)]
                m = [[None] * 3 for _ in range(3)]
                rest, flux = [], []
                for i in range(3):
                    ui = u[i, r, :]
                    th = jnp.tanh(ui)
                    m[i][i] = s + vol * (1.0 + 0.5 * (1.0 - th * th))
                    rest_i = mob[i] * q - source[i, r, :]
                    if not first:
                        old = state[i, r, :]
                        rest_i = rest_i + vol * ((ui - old) + 0.5 * (th - jnp.tanh(old)))
                    rest.append(rest_i)
                    flux.append(s * ui - nu[i, r, :])
                cmat = [[None] * 3 for _ in range(3)]
                for i, (a, b) in enumerate(PAIRS):
                    m[a][b] = s * cp[i]
                    cmat[a][b] = cp[i]
                for i in range(3):
                    m[i][0] = m[i][0] + wc * mob[i]

                def minor(a, b):
                    ra = [i for i in range(3) if i != a]
                    cb = [i for i in range(3) if i != b]
                    v = m[ra[0]][cb[0]] * m[ra[1]][cb[1]]
                    v2 = m[ra[0]][cb[1]] * m[ra[1]][cb[0]]
                    return v - v2 if (a + b) % 2 == 0 else v2 - v
                cof = [[minor(a, b) for b in range(3)] for a in range(3)]
                det = m[0][0] * cof[0][0] + m[0][1] * cof[0][1] + m[0][2] * cof[0][2]
                fac = 1.0 / det
                for i in range(3):
                    inv = [cof[j][i] * fac for j in range(3)]
                    prod = []
                    for j in range(3):
                        v = inv[j]
                        for k in range(3):
                            if k != j:
                                v = v + inv[k] * cmat[k][j]
                        prod.append(v)
                        mm[3 * i + j, r, :] = v
                    ci = -(inv[0] * rest[0] + inv[1] * rest[1] + inv[2] * rest[2]
                           + prod[0] * flux[0] + prod[1] * flux[1] + prod[2] * flux[2])
                    cc[i, r, :] = ci
                    ww[i, r, :] = inv[0] * mob[0] + inv[1] * mob[1] + inv[2] * mob[2]
                    du[slot, i, r, :] = ci
                    t, j = spot(i, z, h)
                    acc[t] = pack(acc[t], ci, j)
            return tuple(acc)
        z0 = jnp.zeros((8, 128), F32)
        acc = lax.fori_loop(0, nz, body, (z0, z0))
        sx[slot] = jnp.concatenate(acc, 0)

    def advance(slot, other, active):
        halo_z(slot)
        xs = halo_x(slot)

        def body(z, acc):
            acc = list(acc)
            for h in range(half):
                r = pl.ds(pl.multiple_of(z * ny + h * 8, 8), 8)
                n = [with_halo(slot, xs, c, z, h) for c in range(3)]
                lf = lfield[r, :]
                for i in range(3):
                    v = (cc[i, r, :] + ww[i, r, :] * lf + mm[3 * i, r, :] * n[0]
                         + mm[3 * i + 1, r, :] * n[1] + mm[3 * i + 2, r, :] * n[2])
                    v = jnp.where(active, v, du[slot, i, r, :])
                    du[other, i, r, :] = v
                    t, j = spot(i, z, h)
                    acc[t] = pack(acc[t], v, j)
            return tuple(acc)
        z0 = jnp.zeros((8, 128), F32)
        acc = lax.fori_loop(0, nz, body, (z0, z0), unroll=2)
        sx[other] = jnp.concatenate(acc, 0)

    base = 0
    for newton in range(NEWTON):
        count = turns[newton]
        f_s = [p[1 + newton:2 + newton] for p in par]
        f_w = well_col(lambda w: controls[0, 0, newton, w].astype(F32))
        consts = [parts(f_s[t], pw_s[t], tgt_s[t], rate_s[t], store_s[t], p0_s[t], rsum_s[t])
                  for t in range(tiles)]
        setup(newton == 0, (base + 1) % 2)
        turns_v = jnp.full((8, 128), iters[newton], jnp.int32)
        turns_g = jnp.full((peers, 128), iters[newton], jnp.int32)

        def slot_dw(gslot, k, consts=consts, turns_g=turns_g):
            for t in range(tiles):
                got = read_g(gbuf, pl.multiple_of(gslot * peers * 8, 8), t)
                gkeep[pl.ds(t * peers, peers), :] = jnp.where(turns_g >= k, got, kept(t))
            sums = same_well(kept)
            return [consts[t][0] + consts[t][1] * sums[t] for t in range(tiles)]

        def share_g(gslot, slot, u0s=u0s):
            got = pick(du[slot, 0])
            now = [u0s[t] + got[t] for t in range(tiles)]
            share([coef[t] * now[t] for t in range(tiles)], gsend.at[gslot], grow(gslot)(me))
            gcopy(gslot, "start")
            return now

        def sweep(k, carry, base=base, turns_v=turns_v):
            slot, other = (base + k) % 2, (base + k + 1) % 2
            put_y(slot, lambda c, y: du[slot, c, pl.ds(y, nz, stride=ny), :])
            copies = halo(slot, du.at[slot])
            start(copies)
            share_g((base + k) % GDEPTH, slot)
            local(lambda c, at: du[slot, c, at, :])
            before = (base + k + GDEPTH - 1) % GDEPTH
            gcopy(before, "wait")
            dw = slot_dw(before, k)
            lfield[...] = scatter([wi_row[t] * dw[t] for t in range(tiles)])
            finish(copies)
            advance(slot, other, turns_v > k)
            return carry

        lax.fori_loop(1, count, sweep, 0)
        last = (base + count) % 2
        if newton < NEWTON - 1:
            put_y(last, lambda c, y: du[last, c, pl.ds(y, nz, stride=ny), :])
            copies = halo(last, du.at[last])
            start(copies)
            u0s = share_g((base + count) % GDEPTH, last)
            local(lambda c, at: du[last, c, at, :])
        before = (base + count - 1) % GDEPTH
        gcopy(before, "wait")
        dw = slot_dw(before, count)
        e_w, k_w = parts(f_w, pw_w, tgt_w, rate_w, store_w, p0_w, rsum_w)
        pw_w = pw_w + (e_w + k_w * own_wells(kept))
        pw_s = [pw_s[t] + dw[t] for t in range(tiles)]
        for c in range(3):
            u[c] = u[c] + du[last, c]
        if newton < NEWTON - 1:
            finish(copies)
            add_to_nu(last, False)
        base += count
    spread_w = jnp.where(well_sub == iota((wells, 128), 1), pw_w, 0.0)
    bhp[...] = jnp.sum(spread_w, axis=0, keepdims=True)


def run(cfg, operands):
    ngx, ngy, ngz, nz, ny, nx, slots, wells, turns = cfg
    peers = ngy * ngz
    rows = nz * ny
    cap = slots // peers
    tiles = operands[6].shape[0] // 8
    V = lambda *shape: pltpu.VMEM(shape, F32)
    vmem = pl.BlockSpec(memory_space=pltpu.VMEM)
    smem = pl.BlockSpec(memory_space=pltpu.SMEM)
    scratch = [
        V(rows, 128), V(rows, 128), V(rows + ny, 128), V(2, ny, 128), V(2, nz, 128), V(2, 8, 128),
        V(rows, 128), V(3, rows, 128), V(3, rows, 128), V(9, rows, 128), V(3, rows, 128),
        V(2, 3, rows, 128), V(3, rows, 128), V(rows, 128), V(rows, 128),
        V(3, 2, 16, 128), V(3, 2, 3 * nz, 128), V(3, 2, 3, ny, 128), V(2, 8, 128), V(2, nz, 128),
        V(2, ny, 128), V(3, 16, 128), V(3, 2, 3 * nz, 128), V(8, 128), V(2, nz, 128),
        V(GDEPTH * peers * 8, 128), V(GDEPTH, 8, 128), V(peers * 8, 128), V(8, 128),
        V(peers * 8 * tiles, 128), V(8 * tiles, 128), V(peers * tiles, 128),
        V(tiles, 2 * cap - 1, peers, 128), V(peers * tiles, 128),
        pltpu.SemaphoreType.DMA((4, 6)), pltpu.SemaphoreType.DMA((4, 6)),
        pltpu.SemaphoreType.DMA((GDEPTH, peers)), pltpu.SemaphoreType.DMA((GDEPTH, peers)),
        pltpu.SemaphoreType.DMA((2, peers)), pltpu.SemaphoreType.DMA((2, peers)),
    ]
    n0, n1 = turns
    return pl.pallas_call(
        functools.partial(kernel, cfg),
        out_shape=(jax.ShapeDtypeStruct((3, rows, 128), F32), jax.ShapeDtypeStruct((1, 128), F32)),
        in_specs=[vmem] * 7 + [smem] * 6,
        out_specs=(vmem, vmem),
        scratch_shapes=scratch,
        compiler_params=pltpu.CompilerParams(
            collective_id=n0 * (ITMAX + 1) + n1 - 2 * (ITMAX + 1) - 2, has_side_effects=True,
            vmem_limit_bytes=48 * 1024 * 1024),
    )(*operands)


def shards(mesh, state_old, source, volume, perm, coupling, mobility, send_cell, send_wi, recv_well,
           controls, inner_iters, well_target, well_rate, well_store, well_pressure):
    ngx, ngy, ngz = mesh.shape["gx"], mesh.shape["gy"], mesh.shape["gz"]
    nz, ny, nx = volume.shape
    slots = send_cell.shape[2]
    wells = well_pressure.shape[2]
    tiles = -(-slots // 128)
    padded = tiles * 128 - slots

    def line(x, fill):
        x = x.reshape(slots).astype(F32)
        return jnp.pad(x, (0, padded), constant_values=fill).reshape(tiles, 1, 128)

    small = jnp.concatenate(
        [line(send_cell, -1.0), line(send_wi, 0.0), line(recv_well, -1.0),
         jnp.zeros((tiles, 5, 128), F32)], axis=1).reshape(tiles * 8, 128)
    flat = lambda x: x.reshape(x.shape[:-3] + (nz * ny, nx))
    operands = (flat(state_old), flat(source), flat(volume), flat(perm), flat(coupling),
                flat(mobility), small, controls, inner_iters, well_target, well_rate, well_store,
                well_pressure)
    tops = (3, 5, ITMAX)
    cases = [(ITMAX, k) for k in tops] + [(k, ITMAX) for k in tops[:-1]]
    n0, n1 = inner_iters[0], inner_iters[1]
    level = lambda n: (n > tops[0]).astype(jnp.int32) + (n > tops[1]).astype(jnp.int32)
    which = jnp.where(n0 > tops[1], level(n1), len(tops) + level(n0))
    which = jnp.where((n1 > tops[1]) | (n0 > tops[1]), which, len(tops) - 1)

    def branch(turns):
        cfg = (ngx, ngy, ngz, nz, ny, nx, slots, wells, turns)
        return lambda *ops: run(cfg, ops)
    cell, bhp = lax.switch(which, [branch(t) for t in cases], *operands)
    return cell.reshape(3, nz, ny, nx), bhp[:, :wells].reshape(1, 1, wells)


def solution(mesh):
    field = P(None, "gz", "gy", "gx")
    peer = P("gx", ("gy", "gz"), None)
    placed = (field, field, P("gz", "gy", "gx"), field, field, field, peer, peer, peer,
              P("gx", ("gy", "gz"), None, None), P(), peer, peer, peer, peer)
    return jax.shard_map(functools.partial(shards, mesh), mesh=mesh, in_specs=placed,
                         out_specs=(field, peer), check_vma=False)
```
